1024 devices in a mesh: wide: 64 (over x, z), cross: 16 (over y, core).
Axes of the slice: x: 8, y: 8, z: 8, core: 2. Of those that a mesh axis runs over, the one named last changes fastest.
Arguments:
- populations: float32 [19, 1024, 8192], P(None, 'wide', 'cross'), may hold values from 0.019 to 0.44, as said below
- relaxation: float32 [1024, 8192], P('wide', 'cross'), may hold values from 0.5 to 1.5
- link_flags: int32 [2, 1024, 8192], P(None, 'wide', 'cross'), may hold values from 0 to 1023, as said below
- migrations: int32 [64, 16, 2], P('wide', 'cross'), may hold values from -1 to 1, as said below
Outputs:
- final_state: float32 [19, 1024, 8192], P(None, 'wide', 'cross')
- guest_block: float32 [19, 1024, 4096], P(None, 'wide', 'cross')
The draws below stay inside these ranges and needn't reach their ends.
Inputs may be any that keep to these rules, and one draw needn't show every extreme that they name: `populations`: populations lie within 0.7 to 1.3 times their lattice weight. `link_flags`: bits agree with the solid cells: a population's bit is set exactly where the cell it pulls from is solid or outside the lattice. `migrations`: entry 0 is a block index below 2, entry 1 is -1, 0 or 1; no device sends past the ends of the wide axis, and no device receives more than one block.
All inputs are finite; a program needn't handle non-finite values.
Results may differ from the reference program's by a relative error of at most 0.00012.
Values sent between devices are 32-bit elements; how exact they have to be, the bound alone decides.
A program may use at most 64 MiB of HBM per device.

```python
import math
import jax
import jax.numpy as jnp
from jax import lax

BLOCK = 16
BZ = 2
STEPS = 3
NX = 1024
NY = 256
NZ = 32
N_WIDE = 64
N_CROSS = 16


VELOCITY = ((0, 0, 0), (1, 0, 0), (-1, 0, 0), (0, 1, 0), (0, -1, 0), (0, 0, 1), (0, 0, -1), (1, 1, 0), (-1, -1, 0), (1, -1, 0), (-1, 1, 0), (1, 0, 1), (-1, 0, -1), (1, 0, -1), (-1, 0, 1), (0, 1, 1), (0, -1, -1), (0, 1, -1), (0, -1, 1))


LATTICE_WEIGHT = (1.0 / 3.0,) + (1.0 / 18.0,) * 6 + (1.0 / 36.0,) * 12


def draw_populations(key, part):
    key = jax.random.fold_in(key, 11)
    shape = (19, NX, NY * BLOCK * BZ)
    weights = jnp.array(LATTICE_WEIGHT, dtype=jnp.float32)
    noise = jax.random.uniform(key, shape, jnp.float32, -0.3, 0.3)
    return weights[:, None, None] * (1.0 + noise)


def draw_link_flags(key, part):
    key = jax.random.fold_in(key, 23)
    depth = BLOCK * BZ
    solid = jax.random.randint(key, (NX, NY, depth), 0, 4) == 0
    xs = lax.broadcasted_iota(jnp.int32, (NX, NY, depth), 0)
    ys = lax.broadcasted_iota(jnp.int32, (NX, NY, depth), 1)
    solid = solid | (xs < 2) | (xs >= NX - 2) | (ys < 2) | (ys >= NY - 2)
    solid_int = solid.astype(jnp.int32)
    padded = jnp.pad(solid_int, 1, constant_values=1)
    low = solid_int
    high = jnp.zeros_like(solid_int)
    for number in range(1, 19):
        step_x, step_y, step_z = VELOCITY[number]
        neighbour = padded[1 - step_x:1 - step_x + NX, 1 - step_y:1 - step_y + NY, 1 - step_z:1 - step_z + depth]
        if number < 10:
            low = low + neighbour * 2 ** number
        else:
            high = high + neighbour * 2 ** (number - 10)
    return jnp.stack([low, high]).reshape(2, NX, NY * depth).astype(jnp.int32)


def draw_migrations(key, part):
    key = jax.random.fold_in(key, 37)
    first_key, second_key = jax.random.split(key)
    chosen = jax.random.randint(first_key, (N_WIDE, N_CROSS), 0, BZ)
    heading = jax.random.randint(second_key, (N_WIDE, N_CROSS), 0, 3) - 1
    position = lax.broadcasted_iota(jnp.int32, (N_WIDE, N_CROSS), 0)
    heading = jnp.where((position == 0) & (heading == -1), 0, heading)
    heading = jnp.where((position == N_WIDE - 1) & (heading == 1), 0, heading)
    heading = heading.at[N_WIDE - 1, 0].set(-1)
    heading = heading.at[N_WIDE - 3, 0].set(0)
    earlier = jnp.concatenate([jnp.zeros((2, N_CROSS), jnp.int32), heading[:-2]], axis=0)
    heading = jnp.where((heading == -1) & (earlier == 1), 0, heading)
    chosen = chosen.at[0, 0].set(BZ - 1)
    return jnp.stack([chosen, heading], axis=-1).astype(jnp.int32)


def steps_of(rng, extent, cuts, smallest, largest):
    def one(dim, shards_of):
        heights = jax.random.uniform(jax.random.fold_in(jax.random.fold_in(rng, 6), dim), (shards_of,), jnp.float32, smallest / len(cuts), largest / len(cuts))
        return jnp.repeat(jnp.exp(heights), extent[dim] // shards_of).reshape((-1,) + (1,) * (len(extent) - dim - 1))

    level = one(*cuts[0])
    for cut in cuts[1:]:
        level = level * one(*cut)
    return level


def setup_inputs(seed: int = 0) -> dict:
    seeds = jax.random.split(jax.random.key(seed), 5)
    return {
        "populations": draw_populations(jax.random.fold_in(seeds[4], 71), 0),
        "relaxation": jnp.clip(jnp.exp(math.log(1.5) - 1.0986123 * jax.random.uniform(seeds[1], (NX, NY * NZ), jnp.float32) ** steps_of(seeds[1], (NX, NY * NZ), ((0, 64), (1, 16)), -0.2, 0.2)), 0.5, 1.5),
        "link_flags": draw_link_flags(jax.random.fold_in(seeds[4], 71), 0),
        "migrations": draw_migrations(jax.random.fold_in(seeds[4], 71), 0),
    }


VELOCITY = ((0, 0, 0), (1, 0, 0), (-1, 0, 0), (0, 1, 0), (0, -1, 0), (0, 0, 1), (0, 0, -1),
            (1, 1, 0), (-1, -1, 0), (1, -1, 0), (-1, 1, 0), (1, 0, 1), (-1, 0, -1), (1, 0, -1),
            (-1, 0, 1), (0, 1, 1), (0, -1, -1), (0, 1, -1), (0, -1, 1))
OPPOSITE = (0, 2, 1, 4, 3, 6, 5, 8, 7, 10, 9, 12, 11, 14, 13, 16, 15, 18, 17)
LATTICE_WEIGHT = (1.0 / 3.0,) + (1.0 / 18.0,) * 6 + (1.0 / 36.0,) * 12


def collide(state, relaxation, fluid):
    density = jnp.sum(state, axis=0)
    divisor = jnp.where(fluid, density, 1.0)
    moments = []
    for axis_number in range(3):
        total = jnp.zeros_like(density)
        for number in range(19):
            factor = VELOCITY[number][axis_number]
            if factor != 0:
                total = total + factor * state[number]
        moments.append(total / divisor)
    square = moments[0] * moments[0] + moments[1] * moments[1] + moments[2] * moments[2]
    result = []
    for number in range(19):
        project = jnp.zeros_like(density)
        for axis_number in range(3):
            factor = VELOCITY[number][axis_number]
            if factor != 0:
                project = project + factor * moments[axis_number]
        balance = LATTICE_WEIGHT[number] * density * (1.0 + 3.0 * project + 4.5 * project * project - 1.5 * square)
        result.append(jnp.where(fluid, state[number] + relaxation * (balance - state[number]), 0.0))
    return jnp.stack(result)


def shift_depth(plane, offset):
    if offset == 1:
        return jnp.concatenate([jnp.zeros_like(plane[..., :1]), plane[..., :-1]], axis=-1)
    if offset == -1:
        return jnp.concatenate([plane[..., 1:], jnp.zeros_like(plane[..., :1])], axis=-1)
    return plane


def stream(padded, post, flags_low, flags_high, fluid, width, height):
    result = []
    for number in range(19):
        step_x, step_y, step_z = VELOCITY[number]
        pulled = padded[number, 1 - step_x:1 - step_x + width, 1 - step_y:1 - step_y + height]
        pulled = shift_depth(pulled, step_z)
        if number < 10:
            blocked = jnp.bitwise_and(jnp.right_shift(flags_low, number), 1) == 1
        else:
            blocked = jnp.bitwise_and(jnp.right_shift(flags_high, number - 10), 1) == 1
        value = jnp.where(blocked, post[OPPOSITE[number]], pulled)
        result.append(jnp.where(fluid, value, 0.0))
    return jnp.stack(result)


def reference(populations, relaxation, link_flags, migrations):
    depth = BLOCK * BZ
    state = populations.reshape(19, NX, NY, depth)
    relax = relaxation.reshape(NX, NY, depth)
    flags_low = link_flags[0].reshape(NX, NY, depth)
    flags_high = link_flags[1].reshape(NX, NY, depth)
    fluid = jnp.bitwise_and(flags_low, 1) == 0
    for step_number in range(STEPS):
        post = collide(state, relax, fluid)
        padded = jnp.pad(post, ((0, 0), (1, 1), (1, 1), (0, 0)))
        state = stream(padded, post, flags_low, flags_high, fluid, NX, NY)
    chosen_index = migrations[:, :, 0]
    heading = migrations[:, :, 1]
    view = state.reshape(19, N_WIDE, BLOCK, N_CROSS, BLOCK, BZ, BLOCK)
    blocks = jnp.transpose(view, (1, 3, 5, 0, 2, 4, 6))
    chosen = jnp.take_along_axis(blocks, chosen_index[:, :, None, None, None, None, None].astype(jnp.int32), axis=2)[:, :, 0]
    eastward = jnp.where((heading == 1)[:, :, None, None, None, None], chosen, 0.0)
    westward = jnp.where((heading == -1)[:, :, None, None, None, None], chosen, 0.0)
    pad_spec_front = ((1, 0), (0, 0), (0, 0), (0, 0), (0, 0), (0, 0))
    pad_spec_back = ((0, 1), (0, 0), (0, 0), (0, 0), (0, 0), (0, 0))
    guests = jnp.pad(eastward, pad_spec_front)[:N_WIDE] + jnp.pad(westward, pad_spec_back)[1:]
    guest_block = jnp.transpose(guests, (2, 0, 3, 1, 4, 5)).reshape(19, NX, NY * BLOCK)
    layer = jnp.arange(BZ, dtype=jnp.int32)
    departed = (layer[None, None, :] == chosen_index[:, :, None]) & (heading != 0)[:, :, None]
    final_state = jnp.where(departed[None, :, None, :, None, :, None], 0.0, view).reshape(19, NX, NY * depth)
    return final_state, guest_block
```

```python
import jax
import jax.numpy as jnp
from jax import lax
from jax.experimental import pallas as pl
from jax.experimental.pallas import tpu as pltpu
from jax.sharding import PartitionSpec as P

MESH = pl.DeviceIdType.MESH
BLOCK = 16
DEPTH = 32
STEPS = 3
ROWS = 16
SPAN = 512
LANES = 128

VELOCITY = (
    (0, 0, 0),
    (1, 0, 0),
    (-1, 0, 0),
    (0, 1, 0),
    (0, -1, 0),
    (0, 0, 1),
    (0, 0, -1),
    (1, 1, 0),
    (-1, -1, 0),
    (1, -1, 0),
    (-1, 1, 0),
    (1, 0, 1),
    (-1, 0, -1),
    (1, 0, -1),
    (-1, 0, 1),
    (0, 1, 1),
    (0, -1, -1),
    (0, 1, -1),
    (0, -1, 1),
)
OPPOSITE = (0, 2, 1, 4, 3, 6, 5, 8, 7, 10, 9, 12, 11, 14, 13, 16, 15, 18, 17)
PAIRS = tuple((q, q + 1) for q in range(1, 19, 2))
CROSS_X = ((1, 7, 9, 11, 13), (2, 8, 10, 12, 14))
CROSS_Y = ((3, 7, 10, 15, 17), (4, 8, 9, 16, 18))
SIGN = (1, -1)
TILES = tuple((q, row, col) for q in range(19) for row in range(2) for col in range(2))


def touched(tile):
    q, row, col = tile
    step_x, step_y, _ = VELOCITY[q]
    return step_x == 1 - 2 * row or step_y == 1 - 2 * col


EARLY = tuple(t for t in TILES if not touched(t))
LATE = tuple(t for t in TILES if touched(t))
ORDER = EARLY + LATE
PLACE = {t: i for i, t in enumerate(ORDER)}


def blocked_bits(flags, q, rows, lanes):
    plane, bit = (0, q) if q < 10 else (1, q - 10)
    return jnp.bitwise_and(flags[plane, rows, lanes], 1 << bit) != 0


def collide(state, relax, post):
    def group(number, carry):
        rows = pl.ds(pl.multiple_of((number // 4) * 8, 8), 8)
        lanes = pl.ds(pl.multiple_of((number % 4) * LANES, LANES), LANES)
        f = [state[q, rows, lanes] for q in range(19)]
        rate = relax[rows, lanes]
        diff = {a: f[a] - f[b] for a, b in PAIRS}
        rho = f[0]
        for a, b in PAIRS:
            rho = rho + (f[a] + f[b])
        scale = 3.0 / rho
        ux = (diff[1] + diff[7] + diff[9] + diff[11] + diff[13]) * scale
        uy = (diff[3] + diff[7] - diff[9] + diff[15] + diff[17]) * scale
        uz = (diff[5] + diff[11] - diff[13] + diff[15] - diff[17]) * scale
        base = 1.0 - (ux * ux + uy * uy + uz * uz) * (1.0 / 6.0)
        keep = 1.0 - rate
        mass = rate * rho
        post[0, rows, lanes] = keep * f[0] + (mass * (1.0 / 3.0)) * base
        axis = mass * (1.0 / 18.0)
        edge = mass * (1.0 / 36.0)
        for a, b in PAIRS:
            cx, cy, cz = VELOCITY[a]
            along = None
            for c, u in ((cx, ux), (cy, uy), (cz, uz)):
                if c != 0:
                    along = u if along is None else (along + u if c > 0 else along - u)
            weight = axis if a < 7 else edge
            even = weight * (base + 0.5 * (along * along))
            odd = weight * along
            post[a, rows, lanes] = keep * f[a] + (even + odd)
            post[b, rows, lanes] = keep * f[b] + (even - odd)
        return carry

    lax.fori_loop(0, 8, group, 0)


def rolled(value, amount, axis):
    amount = amount % value.shape[axis]
    return value if amount == 0 else pltpu.roll(value, amount, axis)


def kernel(
    populations, relaxation, link_flags, migrations, final, guest,
    state, post, relax, flags,
    x_out, x_in, y_out, y_in, c_in,
    east_out, west_out, east_in, west_in,
    load_sem, halo_send, halo_recv, move_send, move_recv,
):
    w = lax.axis_index("wide")
    k = lax.axis_index("cross")
    n_wide = lax.axis_size("wide")
    n_cross = lax.axis_size("cross")
    wide = (lax.rem(w + 1, n_wide), lax.rem(w + n_wide - 1, n_wide))
    cross = (lax.rem(k + 1, n_cross), lax.rem(k + n_cross - 1, n_cross))
    partners = [(wide[0], k), (wide[1], k), (w, cross[0]), (w, cross[1])]
    partners += [(wide[i], cross[j]) for i in range(2) for j in range(2)]

    loads = [
        pltpu.make_async_copy(populations, state, load_sem.at[0]),
        pltpu.make_async_copy(relaxation, relax, load_sem.at[1]),
        pltpu.make_async_copy(link_flags, flags, load_sem.at[2]),
    ]
    for load in loads:
        load.start()
    barrier = pltpu.get_barrier_semaphore()
    for partner in partners:
        pl.semaphore_signal(barrier, inc=1, device_id=partner, device_id_type=MESH)
    for load in loads:
        load.wait()

    lane = lax.broadcasted_iota(jnp.int32, (ROWS, LANES), 1)
    line = lax.broadcasted_iota(jnp.int32, (8, SPAN), 0)
    corner_lane = lax.broadcasted_iota(jnp.int32, (1, SPAN), 1)
    chosen = migrations[0, 0, 0]
    heading = migrations[0, 0, 1]
    whole = slice(None)

    def sends(step):
        copies = []
        for i in range(2):
            copies.append((x_out.at[step, i], x_in.at[step, i]))
        for i in range(2):
            copies.append((y_out.at[step, i], y_in.at[step, i]))
        for i in range(2):
            for j in range(2):
                lanes = pl.ds(0 if j == 0 else SPAN - LANES, LANES)
                copies.append((x_out.at[step, i, :, lanes], c_in.at[step, 2 * i + j]))
        return [
            pltpu.make_async_remote_copy(
                src_ref=source,
                dst_ref=target,
                send_sem=halo_send.at[step, number],
                recv_sem=halo_recv.at[step, number],
                device_id=partners[number],
                device_id_type=MESH,
            )
            for number, (source, target) in enumerate(copies)
        ]

    def faces(step):
        for i in range(2):
            for j, q in enumerate(CROSS_X[i]):
                _, cy, cz = VELOCITY[q]
                rows = slice(8, 16) if i == 0 else slice(0, 8)
                edge = rolled(post[q, rows, :], cy * DEPTH + cz, 1)
                x_out[step, i, j : j + 1, :] = edge[7:8] if i == 0 else edge[0:1]
        for i in range(2):
            packed = [None, None]
            for j, q in enumerate(CROSS_Y[i]):
                cx, cy, cz = VELOCITY[q]
                lanes = slice(SPAN - LANES, SPAN) if i == 0 else slice(0, LANES)
                edge = rolled(post[q, :, lanes], cy * DEPTH + cz + DEPTH * j, 1)
                edge = rolled(edge, cx, 0)
                half = j // 4
                if packed[half] is None:
                    packed[half] = edge
                else:
                    first = (DEPTH * j if i == 0 else DEPTH * j + LANES - DEPTH) % LANES
                    here = (lane >= first) & (lane < first + DEPTH)
                    packed[half] = jnp.where(here, edge, packed[half])
            for half in range(2):
                y_out[step, i, half] = packed[half]

    def stream(last):
        for q in range(19):
            cx, cy, cz = VELOCITY[q]
            value = post[q]
            if q > 0:
                value = rolled(rolled(value, cy * DEPTH + cz, 1), cx, 0)
                value = jnp.where(blocked_bits(flags, q, whole, whole), post[OPPOSITE[q]], value)
            if last:
                value = jnp.where(jnp.bitwise_and(flags[0], 1) == 0, value, 0.0)
            state[q] = value

    def patch(step, last):
        for i in range(2):
            lanes = slice(0, LANES) if i == 0 else slice(SPAN - LANES, SPAN)
            here = lane < DEPTH if i == 0 else lane >= LANES - DEPTH
            for j, q in enumerate(CROSS_Y[i]):
                value = rolled(y_in[step, i, j // 4], -DEPTH * j, 1)
                keep = blocked_bits(flags, q, whole, lanes)
                if last:
                    keep = keep | (jnp.bitwise_and(flags[0, :, lanes], 1) != 0)
                state[q, :, lanes] = jnp.where(here & ~keep, value, state[q, :, lanes])
        for i in range(2):
            rows = slice(0, 8) if i == 0 else slice(8, 16)
            here = line == (0 if i == 0 else 7)
            for j, q in enumerate(CROSS_X[i]):
                value = x_in[step, i, j : j + 1, :]
                cy = VELOCITY[q][1]
                if cy != 0:
                    corner = c_in[step, 2 * i + (0 if cy > 0 else 1), j : j + 1, :]
                    corner = jnp.concatenate([corner] * (SPAN // LANES), axis=1)
                    reach = corner_lane < DEPTH if cy > 0 else corner_lane >= SPAN - DEPTH
                    value = jnp.where(reach, corner, value)
                value = jnp.broadcast_to(value, (8, SPAN))
                keep = blocked_bits(flags, q, rows, whole)
                if last:
                    keep = keep | (jnp.bitwise_and(flags[0, rows, :], 1) != 0)
                state[q, rows, :] = jnp.where(here & ~keep, value, state[q, rows, :])

    for step in range(STEPS):
        last = step == STEPS - 1
        collide(state, relax, post)
        faces(step)
        if step == 0:
            pl.semaphore_wait(barrier, len(partners))
        copies = sends(step)
        for copy in copies:
            copy.start()
        stream(last)
        if last:
            break
        for copy in copies:
            copy.wait()
        patch(step, last)

    tile_lane = lax.broadcasted_iota(jnp.int32, (8, LANES), 1)
    first_pick = (tile_lane % 64) < 16
    second_pick = tile_lane < 32

    def packed_half(q, rows, lanes):
        value = state[q, rows, lanes]
        value = jnp.where(chosen == 1, rolled(value, -BLOCK, 1), value)
        value = jnp.where(first_pick, value, rolled(value, -BLOCK, 1))
        return jnp.where(second_pick, value, rolled(value, -2 * BLOCK, 1))

    def pack(tiles):
        for tile in tiles:
            q, row, col = tile
            rows = slice(8 * row, 8 * row + 8)
            low = packed_half(q, rows, slice(2 * col * LANES, (2 * col + 1) * LANES))
            high = packed_half(q, rows, slice((2 * col + 1) * LANES, (2 * col + 2) * LANES))
            value = jnp.where(tile_lane < 64, low, rolled(high, 64, 1))
            east_out[PLACE[tile]] = jnp.where(heading == 1, value, 0.0)
            west_out[PLACE[tile]] = jnp.where(heading == -1, value, 0.0)

    def moves(part):
        span = pl.ds(0, len(EARLY)) if part == 0 else pl.ds(len(EARLY), len(LATE))
        return [
            pltpu.make_async_remote_copy(
                src_ref=source.at[span],
                dst_ref=target.at[span],
                send_sem=move_send.at[part, number],
                recv_sem=move_recv.at[part, number],
                device_id=(wide[number], k),
                device_id_type=MESH,
            )
            for number, (source, target) in enumerate(((east_out, east_in), (west_out, west_in)))
        ]

    pack(EARLY)
    early = moves(0)
    for copy in early:
        copy.start()
    for copy in copies:
        copy.wait()
    patch(STEPS - 1, True)
    pack(LATE)
    late = moves(1)
    for copy in late:
        copy.start()
    layer = (lax.broadcasted_iota(jnp.int32, (ROWS, SPAN), 1) % DEPTH) // BLOCK
    departed = (layer == chosen) & (heading != 0)
    for q in range(19):
        final[q] = jnp.where(departed, 0.0, state[q])
    for part, copies, tiles in ((0, early, EARLY), (1, late, LATE)):
        for copy in copies:
            copy.wait()
        for tile in tiles:
            q, row, col = tile
            place = PLACE[tile]
            rows = slice(8 * row, 8 * row + 8)
            lanes = slice(col * LANES, (col + 1) * LANES)
            guest[q, rows, lanes] = east_in[place] + west_in[place]


def local(populations, relaxation, link_flags, migrations):
    any_space = pl.BlockSpec(memory_space=pl.ANY)
    vmem = pl.BlockSpec(memory_space=pltpu.VMEM)
    f32 = jnp.float32
    cells = (19, ROWS, SPAN)
    block = (len(TILES), 8, LANES)
    return pl.pallas_call(
        kernel,
        out_shape=(
            jax.ShapeDtypeStruct(cells, f32),
            jax.ShapeDtypeStruct((19, ROWS, SPAN // 2), f32),
        ),
        in_specs=[any_space, any_space, any_space, pl.BlockSpec(memory_space=pltpu.SMEM)],
        out_specs=(vmem, vmem),
        scratch_shapes=[
            pltpu.VMEM(cells, f32),
            pltpu.VMEM(cells, f32),
            pltpu.VMEM((ROWS, SPAN), f32),
            pltpu.VMEM((2, ROWS, SPAN), jnp.int32),
            pltpu.VMEM((STEPS, 2, 8, SPAN), f32),
            pltpu.VMEM((STEPS, 2, 8, SPAN), f32),
            pltpu.VMEM((STEPS, 2, 2, ROWS, LANES), f32),
            pltpu.VMEM((STEPS, 2, 2, ROWS, LANES), f32),
            pltpu.VMEM((STEPS, 4, 8, LANES), f32),
            pltpu.VMEM(block, f32),
            pltpu.VMEM(block, f32),
            pltpu.VMEM(block, f32),
            pltpu.VMEM(block, f32),
            pltpu.SemaphoreType.DMA((3,)),
            pltpu.SemaphoreType.DMA((STEPS, 8)),
            pltpu.SemaphoreType.DMA((STEPS, 8)),
            pltpu.SemaphoreType.DMA((2, 2)),
            pltpu.SemaphoreType.DMA((2, 2)),
        ],
        compiler_params=pltpu.CompilerParams(
            collective_id=0, has_side_effects=True, vmem_limit_bytes=16 * 1024 * 1024
        ),
        cost_estimate=pl.CostEstimate(
            flops=5_000_000, bytes_accessed=2_000_000, transcendentals=0
        ),
    )(populations, relaxation, link_flags, migrations)


def solution(mesh):
    placed = (
        P(None, "wide", "cross"),
        P("wide", "cross"),
        P(None, "wide", "cross"),
        P("wide", "cross", None),
    )
    return jax.shard_map(
        local,
        mesh=mesh,
        in_specs=placed,
        out_specs=(P(None, "wide", "cross"), P(None, "wide", "cross")),
        check_vma=False,
    )
```

```python
import jax
import jax.numpy as jnp
from jax import lax
from jax.experimental import pallas as pl
from jax.experimental.pallas import tpu as pltpu
from jax.sharding import PartitionSpec as P

MESH = pl.DeviceIdType.MESH
BLOCK = 16
DEPTH = 32
ROWS = 16
SPAN = 512
LANES = 128
EXT_ROWS = 24
EXT_SPAN = 768
PLANES = 22
MESSAGE = 56

VELOCITY = (
    (0, 0, 0),
    (1, 0, 0),
    (-1, 0, 0),
    (0, 1, 0),
    (0, -1, 0),
    (0, 0, 1),
    (0, 0, -1),
    (1, 1, 0),
    (-1, -1, 0),
    (1, -1, 0),
    (-1, 1, 0),
    (1, 0, 1),
    (-1, 0, -1),
    (1, 0, -1),
    (-1, 0, 1),
    (0, 1, 1),
    (0, -1, -1),
    (0, 1, -1),
    (0, -1, 1),
)
OPPOSITE = (0, 2, 1, 4, 3, 6, 5, 8, 7, 10, 9, 12, 11, 14, 13, 16, 15, 18, 17)
PAIRS = tuple((q, q + 1) for q in range(1, 19, 2))
CROSS_X = ((1, 7, 9, 11, 13), (2, 8, 10, 12, 14))
CROSS_Y = ((3, 7, 10, 15, 17), (4, 8, 9, 16, 18))
SIGN = (1, -1)
PARTS = ((0, 1, 2, 3, 4), (5, 6, 7, 8, 9), (10, 11, 12, 13, 14), (15, 16, 17, 18))


def blocked_bits(flags, q, rows, lanes):
    plane, bit = (0, q) if q < 10 else (1, q - 10)
    return jnp.bitwise_and(flags[plane, rows, lanes], 1 << bit) != 0


def collide(state, relax, post, across, down):
    def group(number, carry):
        rows = pl.ds(pl.multiple_of((number // across) * 8, 8), 8)
        lanes = pl.ds(pl.multiple_of((number % across) * LANES, LANES), LANES)
        f = [state[q, rows, lanes] for q in range(19)]
        rate = relax[rows, lanes]
        diff = {a: f[a] - f[b] for a, b in PAIRS}
        rho = f[0]
        for a, b in PAIRS:
            rho = rho + (f[a] + f[b])
        scale = 3.0 / rho
        ux = (diff[1] + diff[7] + diff[9] + diff[11] + diff[13]) * scale
        uy = (diff[3] + diff[7] - diff[9] + diff[15] + diff[17]) * scale
        uz = (diff[5] + diff[11] - diff[13] + diff[15] - diff[17]) * scale
        base = 1.0 - (ux * ux + uy * uy + uz * uz) * (1.0 / 6.0)
        keep = 1.0 - rate
        mass = rate * rho
        post[0, rows, lanes] = keep * f[0] + (mass * (1.0 / 3.0)) * base
        axis = mass * (1.0 / 18.0)
        edge = mass * (1.0 / 36.0)
        for a, b in PAIRS:
            cx, cy, cz = VELOCITY[a]
            along = None
            for c, u in ((cx, ux), (cy, uy), (cz, uz)):
                if c != 0:
                    along = u if along is None else (along + u if c > 0 else along - u)
            weight = axis if a < 7 else edge
            even = weight * (base + 0.5 * (along * along))
            odd = weight * along
            post[a, rows, lanes] = keep * f[a] + (even + odd)
            post[b, rows, lanes] = keep * f[b] + (even - odd)
        return carry

    lax.fori_loop(0, across * down, group, 0)


def rolled(value, amount, axis):
    amount = amount % value.shape[axis]
    return value if amount == 0 else pltpu.roll(value, amount, axis)


def streamed(post, flags, batch, rows, lanes):
    values = [post[q] for q in batch]
    values = [
        rolled(v, VELOCITY[q][1] * DEPTH + VELOCITY[q][2], 1) for q, v in zip(batch, values)
    ]
    values = [rolled(v, VELOCITY[q][0], 0)[rows, lanes] for q, v in zip(batch, values)]
    return [
        v
        if q == 0
        else jnp.where(blocked_bits(flags, q, rows, lanes), post[OPPOSITE[q], rows, lanes], v)
        for q, v in zip(batch, values)
    ]


def kernel(
    populations, relaxation, link_flags, migrations, final, guest,
    state, post, relax, flags, move,
    x_out, x_in, c_in, y_in, y_relax, y_flags,
    east_out, west_out, east_in, west_in,
    load_sem, halo_send, halo_recv, move_send, move_recv,
):
    w = lax.axis_index("wide")
    k = lax.axis_index("cross")
    n_wide = lax.axis_size("wide")
    n_cross = lax.axis_size("cross")
    wide = (lax.rem(w + 1, n_wide), lax.rem(w + n_wide - 1, n_wide))
    cross = (lax.rem(k + 1, n_cross), lax.rem(k + n_cross - 1, n_cross))
    in_wide = (w < n_wide - 1, w > 0)
    in_cross = (k < n_cross - 1, k > 0)
    partners = [(wide[0], k), (wide[1], k), (w, cross[0]), (w, cross[1])]
    exists = [in_wide[0], in_wide[1], in_cross[0], in_cross[1]]
    for i in range(2):
        for j in range(2):
            partners.append((wide[i], cross[j]))
            exists.append(jnp.logical_and(in_wide[i], in_cross[j]))
    behind = [exists[n] for n in (1, 0, 3, 2, 7, 6, 5, 4)]

    own_rows, own_lanes = slice(0, ROWS), slice(0, SPAN)
    all_rows, all_lanes = slice(0, EXT_ROWS), slice(0, EXT_SPAN)
    loads = [
        pltpu.make_async_copy(populations, state.at[:, own_rows, own_lanes], load_sem.at[0]),
        pltpu.make_async_copy(relaxation, relax.at[own_rows, own_lanes], load_sem.at[1]),
        pltpu.make_async_copy(link_flags, flags.at[:, own_rows, own_lanes], load_sem.at[2]),
        pltpu.make_async_copy(migrations, move, load_sem.at[3]),
    ]
    for load in loads:
        load.start()
    barrier = pltpu.get_barrier_semaphore()
    for partner, there in zip(partners, exists):

        @pl.when(there)
        def _(partner=partner):
            pl.semaphore_signal(barrier, inc=1, device_id=partner, device_id_type=MESH)

    for load in loads:
        load.wait()

    def remote(source, target, number, partner):
        return pltpu.make_async_remote_copy(
            src_ref=source,
            dst_ref=target,
            send_sem=halo_send.at[number],
            recv_sem=halo_recv.at[number],
            device_id=partner,
            device_id_type=MESH,
        )

    def pack_rows(source, plane):
        x_out[0, 2 * plane : 2 * plane + 2, :] = source[ROWS - 2 : ROWS, own_lanes].astype(jnp.float32)
        x_out[1, 2 * plane : 2 * plane + 2, :] = source[0:2, own_lanes].astype(jnp.float32)

    pack_rows(relax, 19)
    pack_rows(flags.at[0], 20)
    pack_rows(flags.at[1], 21)
    collide(state, relax, post, SPAN // LANES, ROWS // 8)
    for q in range(19):
        pack_rows(post.at[q], q)
    for j in range(5):
        x_out[0, 44 + j : 45 + j, :] = post[CROSS_X[0][j], ROWS - 3 : ROWS - 2, own_lanes]
        x_out[1, 44 + j : 45 + j, :] = post[CROSS_X[1][j], 2:3, own_lanes]

    along_wide = in_wide[0].astype(jnp.int32) + in_wide[1].astype(jnp.int32)
    along_cross = in_cross[0].astype(jnp.int32) + in_cross[1].astype(jnp.int32)
    pl.semaphore_wait(barrier, along_wide + along_cross + along_wide * along_cross)

    last_lanes, first_lanes = slice(SPAN - LANES, SPAN), slice(0, LANES)
    copies = []
    for i in range(2):
        for j, lanes in enumerate((last_lanes, first_lanes)):
            n = 4 + 2 * i + j
            copies.append((n, remote(x_out.at[i, :, lanes], c_in.at[2 * i + j], n, partners[n])))
    for i in range(2):
        copies.append((i, remote(x_out.at[i], x_in.at[i], i, partners[i])))
    for j, lanes in enumerate((last_lanes, first_lanes)):
        n = 2 + j
        copies.append((n, remote(post.at[:, own_rows, lanes], y_in.at[j], n, partners[n])))
        copies.append((n, remote(relax.at[own_rows, lanes], y_relax.at[j], 8 + j, partners[n])))
        copies.append((n, remote(flags.at[:, own_rows, lanes], y_flags.at[j], 10 + j, partners[n])))
    for n, copy in copies:
        pl.when(exists[n])(copy.start)
    for n, copy in copies:
        pl.when(behind[n])(copy.wait_recv)

    for j in range(2):
        lanes = slice(EXT_SPAN - LANES, EXT_SPAN) if j == 0 else slice(SPAN, SPAN + LANES)
        for q in range(19):
            post[q, own_rows, lanes] = y_in[j, q]
        relax[own_rows, lanes] = y_relax[j]
        flags[:, own_rows, lanes] = y_flags[j]

    for i in range(2):
        rows = slice(22, 24) if i == 0 else slice(16, 18)
        third = slice(21, 22) if i == 0 else slice(18, 19)
        pieces = (
            (x_in.at[i], own_lanes),
            (c_in.at[2 * i], slice(EXT_SPAN - LANES, EXT_SPAN)),
            (c_in.at[2 * i + 1], slice(SPAN, SPAN + LANES)),
        )
        for source, lanes in pieces:
            for q in range(19):
                post[q, rows, lanes] = source[2 * q : 2 * q + 2, :]
            relax[rows, lanes] = source[38:40, :]
            for plane in range(2):
                bits = source[40 + 2 * plane : 42 + 2 * plane, :]
                flags[plane, rows, lanes] = bits.astype(jnp.int32)
            for j, q in enumerate(CROSS_X[i]):
                post[q, third, lanes] = source[44 + j : 45 + j, :]

    for n, copy in copies:
        pl.when(exists[n])(copy.wait_send)

    for _ in range(2):
        for batch in ((0,), (1, 2), (3, 4), (5, 6), (7, 8), (9, 10), (11, 12), (13, 14), (15, 16), (17, 18)):
            for q, value in zip(batch, streamed(post, flags, batch, all_rows, all_lanes)):
                state[q] = value
        collide(state, relax, post, EXT_SPAN // LANES, EXT_ROWS // 8)

    chosen = move[0, 0, 0]
    heading = move[0, 0, 1]
    tile_lane = lax.broadcasted_iota(jnp.int32, (8, LANES), 1)
    first_pick = (tile_lane % 64) < 16
    second_pick = tile_lane < 32
    layer = (lax.broadcasted_iota(jnp.int32, (ROWS, SPAN), 1) % DEPTH) // BLOCK
    departed = (layer == chosen) & (heading != 0)

    def place(q, row, col):
        return 4 * q + 2 * row + col

    def pack(batch):
        tiles = [(q, row, col) for q in batch for row in range(2) for col in range(2)]
        values = []
        for q, row, col in tiles:
            for half in range(2):
                lanes = pl.ds((2 * col + half) * LANES, LANES)
                values.append(state[q, 8 * row : 8 * row + 8, lanes])
        moved = [rolled(v, -BLOCK, 1) for v in values]
        values = [jnp.where(chosen == 1, m, v) for m, v in zip(moved, values)]
        moved = [rolled(v, -BLOCK, 1) for v in values]
        values = [jnp.where(first_pick, v, m) for m, v in zip(moved, values)]
        moved = [rolled(v, -2 * BLOCK, 1) for v in values]
        values = [jnp.where(second_pick, v, m) for m, v in zip(moved, values)]
        moved = [rolled(v, 64, 1) for v in values[1::2]]
        for tile, low, high in zip(tiles, values[::2], moved):
            value = jnp.where(tile_lane < 64, low, high)
            east_out[place(*tile)] = jnp.where(heading == 1, value, 0.0)
            west_out[place(*tile)] = jnp.where(heading == -1, value, 0.0)

    def moves(part):
        span = pl.ds(4 * PARTS[part][0], 4 * len(PARTS[part]))
        return [
            pltpu.make_async_remote_copy(
                src_ref=source.at[span],
                dst_ref=target.at[span],
                send_sem=move_send.at[part, number],
                recv_sem=move_recv.at[part, number],
                device_id=(wide[number], k),
                device_id_type=MESH,
            )
            for number, (source, target) in enumerate(((east_out, east_in), (west_out, west_in)))
        ]

    started = []
    for part, pops in enumerate(PARTS):
        for begin in range(0, len(pops), 2):
            batch = pops[begin : begin + 2]
            for q, value in zip(batch, streamed(post, flags, batch, own_rows, own_lanes)):
                solid = jnp.bitwise_and(flags[0, own_rows, own_lanes], 1) != 0
                value = jnp.where(solid, 0.0, value)
                state[q, own_rows, own_lanes] = value
                final[q] = jnp.where(departed, 0.0, value)
            pack(batch)
        started.append(moves(part))
        for number, copy in enumerate(started[-1]):
            pl.when(in_wide[number])(copy.start)
    for part, pops in enumerate(PARTS):
        for number, copy in enumerate(started[part]):
            pl.when(in_wide[1 - number])(copy.wait_recv)
        for q in pops:
            for row in range(2):
                for col in range(2):
                    east = jnp.where(in_wide[1], east_in[place(q, row, col)], 0.0)
                    west = jnp.where(in_wide[0], west_in[place(q, row, col)], 0.0)
                    guest[q, 8 * row : 8 * row + 8, col * LANES : (col + 1) * LANES] = east + west
    for pair in started:
        for number, copy in enumerate(pair):
            pl.when(in_wide[number])(copy.wait_send)


def local(populations, relaxation, link_flags, migrations):
    populations, relaxation, link_flags, migrations = (
        pltpu.with_memory_space_constraint(operand, pltpu.HBM)
        for operand in (populations, relaxation, link_flags, migrations)
    )
    hbm = pl.BlockSpec(memory_space=pltpu.HBM)
    vmem = pl.BlockSpec(memory_space=pltpu.VMEM)
    f32, i32 = jnp.float32, jnp.int32
    block = (19 * 4, 8, LANES)
    return pl.pallas_call(
        kernel,
        out_shape=(
            jax.ShapeDtypeStruct((19, ROWS, SPAN), f32),
            jax.ShapeDtypeStruct((19, ROWS, SPAN // 2), f32),
        ),
        in_specs=[hbm] * 4,
        out_specs=(vmem, vmem),
        scratch_shapes=[
            pltpu.VMEM((19, EXT_ROWS, EXT_SPAN), f32),
            pltpu.VMEM((19, EXT_ROWS, EXT_SPAN), f32),
            pltpu.VMEM((EXT_ROWS, EXT_SPAN), f32),
            pltpu.VMEM((2, EXT_ROWS, EXT_SPAN), i32),
            pltpu.SMEM((1, 1, 2), i32),
            pltpu.VMEM((2, MESSAGE, SPAN), f32),
            pltpu.VMEM((2, MESSAGE, SPAN), f32),
            pltpu.VMEM((4, MESSAGE, LANES), f32),
            pltpu.VMEM((2, 19, ROWS, LANES), f32),
            pltpu.VMEM((2, ROWS, LANES), f32),
            pltpu.VMEM((2, 2, ROWS, LANES), i32),
            pltpu.VMEM(block, f32),
            pltpu.VMEM(block, f32),
            pltpu.VMEM(block, f32),
            pltpu.VMEM(block, f32),
            pltpu.SemaphoreType.DMA((4,)),
            pltpu.SemaphoreType.DMA((12,)),
            pltpu.SemaphoreType.DMA((12,)),
            pltpu.SemaphoreType.DMA((len(PARTS), 2)),
            pltpu.SemaphoreType.DMA((len(PARTS), 2)),
        ],
        compiler_params=pltpu.CompilerParams(
            collective_id=0, has_side_effects=True, vmem_limit_bytes=24 * 1024 * 1024
        ),
        cost_estimate=pl.CostEstimate(
            flops=8_000_000, bytes_accessed=2_000_000, transcendentals=0
        ),
    )(populations, relaxation, link_flags, migrations)


def solution(mesh):
    placed = (
        P(None, "wide", "cross"),
        P("wide", "cross"),
        P(None, "wide", "cross"),
        P("wide", "cross", None),
    )
    return jax.shard_map(
        local,
        mesh=mesh,
        in_specs=placed,
        out_specs=(P(None, "wide", "cross"), P(None, "wide", "cross")),
        check_vma=False,
    )
```

```python
import jax
import jax.numpy as jnp
from jax import lax
from jax.experimental import pallas as pl
from jax.experimental.pallas import tpu as pltpu
from jax.sharding import PartitionSpec as P

MESH = pl.DeviceIdType.MESH
BLOCK = 16
DEPTH = 32
ROWS = 16
SPAN = 512
LANES = 128
EXT_ROWS = 24
EXT_SPAN = 768
NEAR_SPAN = 640
PLANES = 22
MESSAGE = 56

VELOCITY = (
    (0, 0, 0),
    (1, 0, 0),
    (-1, 0, 0),
    (0, 1, 0),
    (0, -1, 0),
    (0, 0, 1),
    (0, 0, -1),
    (1, 1, 0),
    (-1, -1, 0),
    (1, -1, 0),
    (-1, 1, 0),
    (1, 0, 1),
    (-1, 0, -1),
    (1, 0, -1),
    (-1, 0, 1),
    (0, 1, 1),
    (0, -1, -1),
    (0, 1, -1),
    (0, -1, 1),
)
OPPOSITE = (0, 2, 1, 4, 3, 6, 5, 8, 7, 10, 9, 12, 11, 14, 13, 16, 15, 18, 17)
PAIRS = tuple((q, q + 1) for q in range(1, 19, 2))
CROSS_X = ((1, 7, 9, 11, 13), (2, 8, 10, 12, 14))
CROSS_Y = ((3, 7, 10, 15, 17), (4, 8, 9, 16, 18))
SIGN = (1, -1)
BATCHES = ((0,),) + PAIRS
INNER = 4
REST = ((0, 1), (1, 0), (1, 1))
PARTS = ((0, 1), (2, 3, 4, 5), (6, 7, 8, 9, 10, 11), (12, 13, 14, 15, 16, 17, 18))


def blocked_bits(flags, q, rows, lanes):
    plane, bit = (0, q) if q < 10 else (1, q - 10)
    return jnp.bitwise_and(flags[plane, rows, lanes], 1 << bit) != 0


def collide(state, relax, post, across, down):
    def group(number, carry):
        rows = pl.ds(pl.multiple_of((number // across) * 8, 8), 8)
        lanes = pl.ds(pl.multiple_of((number % across) * LANES, LANES), LANES)
        f = [state[q, rows, lanes] for q in range(19)]
        rate = relax[rows, lanes]
        diff = {a: f[a] - f[b] for a, b in PAIRS}
        rho = f[0]
        for a, b in PAIRS:
            rho = rho + (f[a] + f[b])
        scale = 3.0 / rho
        ux = (diff[1] + diff[7] + diff[9] + diff[11] + diff[13]) * scale
        uy = (diff[3] + diff[7] - diff[9] + diff[15] + diff[17]) * scale
        uz = (diff[5] + diff[11] - diff[13] + diff[15] - diff[17]) * scale
        base = 1.0 - (ux * ux + uy * uy + uz * uz) * (1.0 / 6.0)
        keep = 1.0 - rate
        mass = rate * rho
        post[0, rows, lanes] = keep * f[0] + (mass * (1.0 / 3.0)) * base
        axis = mass * (1.0 / 18.0)
        edge = mass * (1.0 / 36.0)
        for a, b in PAIRS:
            cx, cy, cz = VELOCITY[a]
            along = None
            for c, u in ((cx, ux), (cy, uy), (cz, uz)):
                if c != 0:
                    along = u if along is None else (along + u if c > 0 else along - u)
            weight = axis if a < 7 else edge
            even = weight * (base + 0.5 * (along * along))
            odd = weight * along
            post[a, rows, lanes] = keep * f[a] + (even + odd)
            post[b, rows, lanes] = keep * f[b] + (even - odd)
        return carry

    lax.fori_loop(0, across * down, group, 0, unroll=5 if across == 5 else 4)


def rolled(value, amount, axis):
    amount = amount % value.shape[axis]
    return value if amount == 0 else pltpu.roll(value, amount, axis)


def streamed(post, flags, batch, height, span, rows, lanes):
    wide = span > lanes.stop > SPAN

    def kept(value):
        if not wide:
            return value[rows, lanes]
        above, below = value[rows, SPAN : SPAN + LANES], value[rows, span - LANES : span]
        here = lax.broadcasted_iota(jnp.int32, above.shape, 1) < 2 * DEPTH
        return jnp.concatenate([value[rows, :SPAN], jnp.where(here, above, below)], axis=1)

    values = [post[q, 0:height, 0:span] for q in batch]
    values = [
        rolled(v, VELOCITY[q][1] * DEPTH + VELOCITY[q][2], 1) for q, v in zip(batch, values)
    ]
    values = [kept(rolled(v, VELOCITY[q][0], 0)) for q, v in zip(batch, values)]
    return [
        v
        if q == 0
        else jnp.where(
            blocked_bits(flags, q, rows, lanes), kept(post[OPPOSITE[q], 0:height, 0:span]), v
        )
        for q, v in zip(batch, values)
    ]


def kernel(
    populations, relaxation, link_flags, migrations, final, guest,
    state, post, inner, inner_post, relax, flags, move,
    x_out, x_in, c_in, y_in, y_relax, y_flags,
    east_out, west_out, east_in, west_in,
    load_sem, halo_send, halo_recv, move_send, move_recv,
):
    w = lax.axis_index("wide")
    k = lax.axis_index("cross")
    n_wide = lax.axis_size("wide")
    n_cross = lax.axis_size("cross")
    wide = (lax.rem(w + 1, n_wide), lax.rem(w + n_wide - 1, n_wide))
    cross = (lax.rem(k + 1, n_cross), lax.rem(k + n_cross - 1, n_cross))
    in_wide = (w < n_wide - 1, w > 0)
    in_cross = (k < n_cross - 1, k > 0)
    partners = [(wide[0], k), (wide[1], k), (w, cross[0]), (w, cross[1])]
    exists = [in_wide[0], in_wide[1], in_cross[0], in_cross[1]]
    for i in range(2):
        for j in range(2):
            partners.append((wide[i], cross[j]))
            exists.append(jnp.logical_and(in_wide[i], in_cross[j]))
    behind = [exists[n] for n in (1, 0, 3, 2, 7, 6, 5, 4)]

    own_rows, own_lanes = slice(0, ROWS), slice(0, SPAN)
    all_rows, near_lanes = slice(0, EXT_ROWS), slice(0, NEAR_SPAN)
    loads = [
        pltpu.make_async_copy(populations, state.at[:, own_rows, own_lanes], load_sem.at[0]),
        pltpu.make_async_copy(relaxation, relax.at[own_rows, own_lanes], load_sem.at[1]),
        pltpu.make_async_copy(link_flags, flags.at[:, own_rows, own_lanes], load_sem.at[2]),
        pltpu.make_async_copy(migrations, move, load_sem.at[3]),
    ]
    for load in loads:
        load.start()
    barrier = pltpu.get_barrier_semaphore()
    for partner, there in zip(partners, exists):

        @pl.when(there)
        def _(partner=partner):
            pl.semaphore_signal(barrier, inc=1, device_id=partner, device_id_type=MESH)

    for load in loads:
        load.wait()

    def remote(source, target, number, partner):
        return pltpu.make_async_remote_copy(
            src_ref=source,
            dst_ref=target,
            send_sem=halo_send.at[number],
            recv_sem=halo_recv.at[number],
            device_id=partner,
            device_id_type=MESH,
        )

    def pack_rows(source, plane):
        x_out[0, 2 * plane : 2 * plane + 2, :] = source[ROWS - 2 : ROWS, own_lanes].astype(jnp.float32)
        x_out[1, 2 * plane : 2 * plane + 2, :] = source[0:2, own_lanes].astype(jnp.float32)

    pack_rows(relax, 19)
    pack_rows(flags.at[0], 20)
    pack_rows(flags.at[1], 21)
    collide(state, relax, post, SPAN // LANES, ROWS // 8)
    for q in range(19):
        pack_rows(post.at[q], q)
    for j in range(5):
        x_out[0, 44 + j : 45 + j, :] = post[CROSS_X[0][j], ROWS - 3 : ROWS - 2, own_lanes]
        x_out[1, 44 + j : 45 + j, :] = post[CROSS_X[1][j], 2:3, own_lanes]

    along_wide = in_wide[0].astype(jnp.int32) + in_wide[1].astype(jnp.int32)
    along_cross = in_cross[0].astype(jnp.int32) + in_cross[1].astype(jnp.int32)
    pl.semaphore_wait(barrier, along_wide + along_cross + along_wide * along_cross)

    last_lanes, first_lanes = slice(SPAN - LANES, SPAN), slice(0, LANES)
    copies = []
    for i in range(2):
        for j, lanes in enumerate((last_lanes, first_lanes)):
            n = 4 + 2 * i + j
            copies.append((n, remote(x_out.at[i, :, lanes], c_in.at[2 * i + j], n, partners[n])))
    for i in range(2):
        copies.append((i, remote(x_out.at[i], x_in.at[i], i, partners[i])))
    for j, lanes in enumerate((last_lanes, first_lanes)):
        n = 2 + j
        copies.append((n, remote(post.at[:, own_rows, lanes], y_in.at[j], n, partners[n])))
        copies.append((n, remote(relax.at[own_rows, lanes], y_relax.at[j], 8 + j, partners[n])))
        copies.append((n, remote(flags.at[:, own_rows, lanes], y_flags.at[j], 10 + j, partners[n])))
    for n, copy in copies:
        pl.when(exists[n])(copy.start)
    chosen = move[0, 0, 0]
    heading = move[0, 0, 1]
    tile_lane = lax.broadcasted_iota(jnp.int32, (8, LANES), 1)
    tile_row = lax.broadcasted_iota(jnp.int32, (8, LANES), 0)
    first_pick = (tile_lane % 64) < 16
    second_pick = tile_lane < 32
    layer = (lax.broadcasted_iota(jnp.int32, (ROWS, SPAN), 1) % DEPTH) // BLOCK
    departed = (layer == chosen) & (heading != 0)

    def place(q, row, col):
        return q if (row, col) == (0, 0) else 19 + 3 * q + REST.index((row, col))

    def pack(source, tiles):
        values = []
        for q, row, col in tiles:
            for number in ((1, 2), (3, 0))[col]:
                lanes = slice(number * LANES, (number + 1) * LANES)
                values.append(source[q, 8 * row : 8 * row + 8, lanes])
        moved = [rolled(v, -BLOCK, 1) for v in values]
        values = [jnp.where(chosen == 1, m, v) for m, v in zip(moved, values)]
        moved = [rolled(v, -BLOCK, 1) for v in values]
        values = [jnp.where(first_pick, v, m) for m, v in zip(moved, values)]
        moved = [rolled(v, -2 * BLOCK, 1) for v in values]
        values = [jnp.where(second_pick, v, m) for m, v in zip(moved, values)]
        moved = [rolled(v, 64, 1) for v in values[1::2]]
        for tile, low, high in zip(tiles, values[::2], moved):
            value = jnp.where(tile_lane < 64, low, high)
            east_out[place(*tile)] = jnp.where(heading == 1, value, 0.0)
            west_out[place(*tile)] = jnp.where(heading == -1, value, 0.0)

    def begin(part, first, count):
        span = pl.ds(first, count)
        pair = [
            pltpu.make_async_remote_copy(
                src_ref=source.at[span],
                dst_ref=target.at[span],
                send_sem=move_send.at[part, number],
                recv_sem=move_recv.at[part, number],
                device_id=(wide[number], k),
                device_id_type=MESH,
            )
            for number, (source, target) in enumerate(((east_out, east_in), (west_out, west_in)))
        ]
        for number, copy in enumerate(pair):
            pl.when(in_wide[number])(copy.start)
        return pair

    def cleared(value):
        return jnp.where(jnp.bitwise_and(flags[0, own_rows, own_lanes], 1) != 0, 0.0, value)

    source = post
    for step in range(3):
        for batch in BATCHES:
            values = streamed(source, flags, batch, ROWS, SPAN, own_rows, own_lanes)
            for q, value in zip(batch, values):
                inner[q] = value if step < 2 else rolled(cleared(value), -INNER, 0)
        if step < 2:
            collide(inner, relax, inner_post, SPAN // LANES, ROWS // 8)
            source = inner_post
    for first in range(0, 19, 10):
        pack(inner, [(q, 0, 0) for q in range(first, min(first + 10, 19))])
    started = [begin(0, 0, 19)]

    for n, copy in copies:
        pl.when(behind[n])(copy.wait_recv)

    for j in range(2):
        lanes = slice(EXT_SPAN - LANES, EXT_SPAN) if j == 0 else slice(SPAN, SPAN + LANES)
        for q in range(19):
            post[q, own_rows, lanes] = y_in[j, q]
    near = slice(SPAN, NEAR_SPAN)

    def merged(above, below):
        here = lax.broadcasted_iota(jnp.int32, above.shape, above.ndim - 1) < 2 * DEPTH
        return jnp.where(here, above, below)

    relax[own_rows, near] = merged(y_relax[1], y_relax[0])
    for plane in range(2):
        flags[plane, own_rows, near] = merged(y_flags[1, plane], y_flags[0, plane])

    for i in range(2):
        rows = slice(22, 24) if i == 0 else slice(16, 18)
        third = slice(21, 22) if i == 0 else slice(18, 19)
        pieces = (
            (x_in.at[i], own_lanes),
            (c_in.at[2 * i], slice(EXT_SPAN - LANES, EXT_SPAN)),
            (c_in.at[2 * i + 1], slice(SPAN, SPAN + LANES)),
        )
        for source, lanes in pieces:
            for q in range(19):
                post[q, rows, lanes] = source[2 * q : 2 * q + 2, :]
            for j, q in enumerate(CROSS_X[i]):
                post[q, third, lanes] = source[44 + j : 45 + j, :]
        pieces = (
            (lambda part: x_in[i, part, :], own_lanes),
            (lambda part: merged(c_in[2 * i + 1, part, :], c_in[2 * i, part, :]), near),
        )
        for source, lanes in pieces:
            relax[rows, lanes] = source(slice(38, 40))
            for plane in range(2):
                bits = source(slice(40 + 2 * plane, 42 + 2 * plane))
                flags[plane, rows, lanes] = bits.astype(jnp.int32)

    for n, copy in copies:
        pl.when(exists[n])(copy.wait_send)

    for span in (EXT_SPAN, NEAR_SPAN):
        for batch in BATCHES:
            for q, value in zip(batch, streamed(post, flags, batch, EXT_ROWS, span, all_rows, near_lanes)):
                state[q, :, near_lanes] = value
        collide(state, relax, post, NEAR_SPAN // LANES, EXT_ROWS // 8)

    for part, pops in enumerate(PARTS):
        for first in range(0, len(pops), 2):
            batch = pops[first : first + 2]
            values = streamed(post, flags, batch, EXT_ROWS, NEAR_SPAN, own_rows, own_lanes)
            for q, value in zip(batch, values):
                value = cleared(value)
                final[q] = jnp.where(departed, 0.0, value)
                state[q, own_rows, own_lanes] = rolled(value, -INNER, 0)
            pack(state, [(q, row, col) for q in batch for row, col in REST])
        started.append(begin(1 + part, 19 + 3 * pops[0], 3 * len(pops)))

    def arrived(part):
        for number, copy in enumerate(started[part]):
            pl.when(in_wide[1 - number])(copy.wait_recv)

    def received(q, row, col):
        east = jnp.where(in_wide[1], east_in[place(q, row, col)], 0.0)
        west = jnp.where(in_wide[0], west_in[place(q, row, col)], 0.0)
        return rolled(east + west, INNER, 0)

    arrived(0)
    for part, pops in enumerate(PARTS):
        arrived(1 + part)
        for first in range(0, len(pops), 2):
            batch = pops[first : first + 2]
            tiles = [[[received(q, row, col) for col in range(2)] for row in range(2)] for q in batch]
            tiles = [
                [
                    [
                        rolled(jnp.where(tile_row < INNER, t[1 - row][col], t[row][col]), 64, 1)
                        for col in range(2)
                    ]
                    for row in range(2)
                ]
                for t in tiles
            ]
            for q, t in zip(batch, tiles):
                for row in range(2):
                    rows = slice(8 * row, 8 * row + 8)
                    guest[q, rows, 0:LANES] = jnp.where(tile_lane < 64, t[row][1], t[row][0])
                    guest[q, rows, LANES:] = jnp.where(tile_lane < 64, t[row][0], t[row][1])
    for pair in started:
        for number, copy in enumerate(pair):
            pl.when(in_wide[number])(copy.wait_send)


def store(final, guest, final_out, guest_out, sems):
    copies = [
        pltpu.make_async_copy(final, final_out, sems.at[0]),
        pltpu.make_async_copy(guest, guest_out, sems.at[1]),
    ]
    for copy in copies:
        copy.start()
    for copy in copies:
        copy.wait()


def local(populations, relaxation, link_flags, migrations):
    populations, relaxation, link_flags, migrations = (
        pltpu.with_memory_space_constraint(operand, pltpu.HBM)
        for operand in (populations, relaxation, link_flags, migrations)
    )
    hbm = pl.BlockSpec(memory_space=pltpu.HBM)
    vmem = pl.BlockSpec(memory_space=pltpu.VMEM)
    f32, i32 = jnp.float32, jnp.int32
    block = (19 * 4, 8, LANES)
    results = pl.pallas_call(
        kernel,
        out_shape=(
            jax.ShapeDtypeStruct((19, ROWS, SPAN), f32),
            jax.ShapeDtypeStruct((19, ROWS, SPAN // 2), f32),
        ),
        in_specs=[hbm] * 4,
        out_specs=(vmem, vmem),
        scratch_shapes=[
            pltpu.VMEM((19, EXT_ROWS, NEAR_SPAN), f32),
            pltpu.VMEM((19, EXT_ROWS, EXT_SPAN), f32),
            pltpu.VMEM((19, ROWS, SPAN), f32),
            pltpu.VMEM((19, ROWS, SPAN), f32),
            pltpu.VMEM((EXT_ROWS, NEAR_SPAN), f32),
            pltpu.VMEM((2, EXT_ROWS, NEAR_SPAN), i32),
            pltpu.SMEM((1, 1, 2), i32),
            pltpu.VMEM((2, MESSAGE, SPAN), f32),
            pltpu.VMEM((2, MESSAGE, SPAN), f32),
            pltpu.VMEM((4, MESSAGE, LANES), f32),
            pltpu.VMEM((2, 19, ROWS, LANES), f32),
            pltpu.VMEM((2, ROWS, LANES), f32),
            pltpu.VMEM((2, 2, ROWS, LANES), i32),
            pltpu.VMEM(block, f32),
            pltpu.VMEM(block, f32),
            pltpu.VMEM(block, f32),
            pltpu.VMEM(block, f32),
            pltpu.SemaphoreType.DMA((4,)),
            pltpu.SemaphoreType.DMA((12,)),
            pltpu.SemaphoreType.DMA((12,)),
            pltpu.SemaphoreType.DMA((1 + len(PARTS), 2)),
            pltpu.SemaphoreType.DMA((1 + len(PARTS), 2)),
        ],
        compiler_params=pltpu.CompilerParams(
            collective_id=0, has_side_effects=True, vmem_limit_bytes=24 * 1024 * 1024
        ),
        cost_estimate=pl.CostEstimate(
            flops=8_000_000, bytes_accessed=2_000_000, transcendentals=0
        ),
    )(populations, relaxation, link_flags, migrations)
    return pl.pallas_call(
        store,
        out_shape=tuple(jax.ShapeDtypeStruct(r.shape, f32) for r in results),
        in_specs=[vmem] * 2,
        out_specs=(hbm, hbm),
        scratch_shapes=[pltpu.SemaphoreType.DMA((2,))],
        compiler_params=pltpu.CompilerParams(vmem_limit_bytes=8 * 1024 * 1024),
    )(*results)


def solution(mesh):
    placed = (
        P(None, "wide", "cross"),
        P("wide", "cross"),
        P(None, "wide", "cross"),
        P("wide", "cross", None),
    )
    return jax.shard_map(
        local,
        mesh=mesh,
        in_specs=placed,
        out_specs=(P(None, "wide", "cross"), P(None, "wide", "cross")),
        check_vma=False,
    )
```

```python
import jax
import jax.numpy as jnp
from jax import lax
from jax.experimental import pallas as pl
from jax.experimental.pallas import tpu as pltpu
from jax.sharding import PartitionSpec as P

MESH = pl.DeviceIdType.MESH
BLOCK = 16
DEPTH = 32
ROWS = 16
SPAN = 512
LANES = 128
EXT_ROWS = 24
EXT_SPAN = 768
NEAR_SPAN = 640
PLANES = 22
MESSAGE = 56
CORNER = 32

VELOCITY = (
    (0, 0, 0),
    (1, 0, 0),
    (-1, 0, 0),
    (0, 1, 0),
    (0, -1, 0),
    (0, 0, 1),
    (0, 0, -1),
    (1, 1, 0),
    (-1, -1, 0),
    (1, -1, 0),
    (-1, 1, 0),
    (1, 0, 1),
    (-1, 0, -1),
    (1, 0, -1),
    (-1, 0, 1),
    (0, 1, 1),
    (0, -1, -1),
    (0, 1, -1),
    (0, -1, 1),
)
OPPOSITE = (0, 2, 1, 4, 3, 6, 5, 8, 7, 10, 9, 12, 11, 14, 13, 16, 15, 18, 17)
PAIRS = tuple((q, q + 1) for q in range(1, 19, 2))
CROSS_X = ((1, 7, 9, 11, 13), (2, 8, 10, 12, 14))
CROSS_Y = ((3, 7, 10, 15, 17), (4, 8, 9, 16, 18))
SHARED = tuple(
    tuple(next(n for n, q in enumerate(xs) if q in ys) for ys in CROSS_Y) for xs in CROSS_X
)
BATCHES = ((0,),) + PAIRS
INNER = 4
REST = ((0, 1), (1, 0), (1, 1))
PARTS = ((0, 1), (2, 3, 4, 5), (6, 7, 8, 9, 10, 11), (12, 13, 14, 15, 16, 17, 18))


def blocked_bits(flags, q, rows, lanes):
    plane, bit = (0, q) if q < 10 else (1, q - 10)
    return jnp.bitwise_and(flags[plane, rows, lanes], 1 << bit) != 0


def collide(state, relax, post, across, down):
    def group(number, carry):
        rows = pl.ds(pl.multiple_of((number // across) * 8, 8), 8)
        lanes = pl.ds(pl.multiple_of((number % across) * LANES, LANES), LANES)
        f = [state[q, rows, lanes] for q in range(19)]
        rate = relax[rows, lanes]
        diff = {a: f[a] - f[b] for a, b in PAIRS}
        rho = f[0]
        for a, b in PAIRS:
            rho = rho + (f[a] + f[b])
        scale = 3.0 / rho
        ux = (diff[1] + diff[7] + diff[9] + diff[11] + diff[13]) * scale
        uy = (diff[3] + diff[7] - diff[9] + diff[15] + diff[17]) * scale
        uz = (diff[5] + diff[11] - diff[13] + diff[15] - diff[17]) * scale
        base = 1.0 - (ux * ux + uy * uy + uz * uz) * (1.0 / 6.0)
        keep = 1.0 - rate
        mass = rate * rho
        post[0, rows, lanes] = keep * f[0] + (mass * (1.0 / 3.0)) * base
        axis = mass * (1.0 / 18.0)
        edge = mass * (1.0 / 36.0)
        for a, b in PAIRS:
            cx, cy, cz = VELOCITY[a]
            along = None
            for c, u in ((cx, ux), (cy, uy), (cz, uz)):
                if c != 0:
                    along = u if along is None else (along + u if c > 0 else along - u)
            weight = axis if a < 7 else edge
            even = weight * (base + 0.5 * (along * along))
            odd = weight * along
            post[a, rows, lanes] = keep * f[a] + (even + odd)
            post[b, rows, lanes] = keep * f[b] + (even - odd)
        return carry

    lax.fori_loop(0, across * down, group, 0, unroll=5 if across == 5 else 4)


def rolled(value, amount, axis):
    amount = amount % value.shape[axis]
    return value if amount == 0 else pltpu.roll(value, amount, axis)


def streamed(post, flags, batch, height, span, rows, lanes):
    wide = span > lanes.stop > SPAN

    def kept(value):
        if not wide:
            return value[rows, lanes]
        above, below = value[rows, SPAN : SPAN + LANES], value[rows, span - LANES : span]
        here = lax.broadcasted_iota(jnp.int32, above.shape, 1) < 2 * DEPTH
        return jnp.concatenate([value[rows, :SPAN], jnp.where(here, above, below)], axis=1)

    values = [post[q, 0:height, 0:span] for q in batch]
    values = [
        rolled(v, VELOCITY[q][1] * DEPTH + VELOCITY[q][2], 1) for q, v in zip(batch, values)
    ]
    values = [kept(rolled(v, VELOCITY[q][0], 0)) for q, v in zip(batch, values)]
    return [
        v
        if q == 0
        else jnp.where(
            blocked_bits(flags, q, rows, lanes), kept(post[OPPOSITE[q], 0:height, 0:span]), v
        )
        for q, v in zip(batch, values)
    ]


def kernel(
    populations, relaxation, link_flags, migrations, final, guest,
    state, post, inner, inner_post, relax, flags, move,
    x_out, x_in, c_out, c_in, c_rows, c_full, y_in, y_relax, y_flags,
    east_out, west_out, east_in, west_in,
    load_sem, halo_send, halo_recv, move_send, move_recv,
):
    w = lax.axis_index("wide")
    k = lax.axis_index("cross")
    n_wide = lax.axis_size("wide")
    n_cross = lax.axis_size("cross")
    wide = (lax.rem(w + 1, n_wide), lax.rem(w + n_wide - 1, n_wide))
    cross = (lax.rem(k + 1, n_cross), lax.rem(k + n_cross - 1, n_cross))
    in_wide = (w < n_wide - 1, w > 0)
    in_cross = (k < n_cross - 1, k > 0)
    partners = [(wide[0], k), (wide[1], k), (w, cross[0]), (w, cross[1])]
    exists = [in_wide[0], in_wide[1], in_cross[0], in_cross[1]]
    for i in range(2):
        for j in range(2):
            partners.append((wide[i], cross[j]))
            exists.append(jnp.logical_and(in_wide[i], in_cross[j]))
    behind = [exists[n] for n in (1, 0, 3, 2, 7, 6, 5, 4)]

    own_rows, own_lanes = slice(0, ROWS), slice(0, SPAN)
    all_rows, near_lanes = slice(0, EXT_ROWS), slice(0, NEAR_SPAN)
    loads = [
        pltpu.make_async_copy(populations, state.at[:, own_rows, own_lanes], load_sem.at[0]),
        pltpu.make_async_copy(relaxation, relax.at[own_rows, own_lanes], load_sem.at[1]),
        pltpu.make_async_copy(link_flags, flags.at[:, own_rows, own_lanes], load_sem.at[2]),
        pltpu.make_async_copy(migrations, move, load_sem.at[3]),
    ]
    for load in loads:
        load.start()
    barrier = pltpu.get_barrier_semaphore()
    for partner, there in zip(partners, exists):

        @pl.when(there)
        def _(partner=partner):
            pl.semaphore_signal(barrier, inc=1, device_id=partner, device_id_type=MESH)

    for load in loads:
        load.wait()

    def remote(source, target, number, partner):
        return pltpu.make_async_remote_copy(
            src_ref=source,
            dst_ref=target,
            send_sem=halo_send.at[number],
            recv_sem=halo_recv.at[number],
            device_id=partner,
            device_id_type=MESH,
        )

    def pack_rows(source, plane):
        x_out[0, 2 * plane : 2 * plane + 2, :] = source[ROWS - 2 : ROWS, own_lanes].astype(jnp.float32)
        x_out[1, 2 * plane : 2 * plane + 2, :] = source[0:2, own_lanes].astype(jnp.float32)

    pack_rows(relax, 19)
    pack_rows(flags.at[0], 20)
    pack_rows(flags.at[1], 21)
    collide(state, relax, post, SPAN // LANES, ROWS // 8)
    for q in range(19):
        pack_rows(post.at[q], q)
    for j in range(5):
        x_out[0, 44 + j : 45 + j, :] = post[CROSS_X[0][j], ROWS - 3 : ROWS - 2, own_lanes]
        x_out[1, 44 + j : 45 + j, :] = post[CROSS_X[1][j], 2:3, own_lanes]

    along_wide = in_wide[0].astype(jnp.int32) + in_wide[1].astype(jnp.int32)
    along_cross = in_cross[0].astype(jnp.int32) + in_cross[1].astype(jnp.int32)
    pl.semaphore_wait(barrier, along_wide + along_cross + along_wide * along_cross)

    last_lanes, first_lanes = slice(SPAN - LANES, SPAN), slice(0, LANES)
    def corner_lanes(j, count):
        lane = lax.broadcasted_iota(jnp.int32, (count, LANES), 1)
        if j == 0:
            return lane >= 2 * DEPTH, (lane >= DEPTH) & (lane < 2 * DEPTH), DEPTH
        return lane < 2 * DEPTH, (lane >= 2 * DEPTH) & (lane < 3 * DEPTH), -DEPTH

    copies = []
    for i in range(2):
        for j, lanes in enumerate((last_lanes, first_lanes)):
            n = 2 * i + j
            near, third, shift = corner_lanes(j, 8)
            for m, q in enumerate(CROSS_Y[j]):
                first = 2 * m if m < 4 else 10
                c_rows[n, first : first + 2, :] = x_out[i, 2 * q : 2 * q + 2, lanes]
            c_rows[n, 8:9, :] = x_out[i, 48:49, lanes]
            c_rows[n, 12:13, :] = x_out[i, 44 + SHARED[i][j] : 45 + SHARED[i][j], lanes]
            for block in range(0, 24, 8):
                high = rolled(x_out[i, 24 + block : 32 + block, lanes], 2 * DEPTH, 1)
                c_out[n, block : block + 8, :] = jnp.where(
                    near, x_out[i, block : block + 8, lanes], high
                )
            c_out[n, 24:32, :] = jnp.where(
                third, c_rows[n, 0:8, :], rolled(c_rows[n, 8:16, :], shift, 1)
            )
            copies.append((4 + n, remote(c_out.at[n], c_in.at[n], 4 + n, partners[4 + n])))
    for i in range(2):
        copies.append((i, remote(x_out.at[i], x_in.at[i], i, partners[i])))
    for j, lanes in enumerate((last_lanes, first_lanes)):
        n = 2 + j
        copies.append((n, remote(post.at[:, own_rows, lanes], y_in.at[j], n, partners[n])))
        copies.append((n, remote(relax.at[own_rows, lanes], y_relax.at[j], 8 + j, partners[n])))
        copies.append((n, remote(flags.at[:, own_rows, lanes], y_flags.at[j], 10 + j, partners[n])))
    for n, copy in copies:
        pl.when(exists[n])(copy.start)
    chosen = move[0, 0, 0]
    heading = move[0, 0, 1]
    tile_lane = lax.broadcasted_iota(jnp.int32, (8, LANES), 1)
    tile_row = lax.broadcasted_iota(jnp.int32, (8, LANES), 0)
    first_pick = (tile_lane % 64) < 16
    second_pick = tile_lane < 32
    layer = (lax.broadcasted_iota(jnp.int32, (ROWS, SPAN), 1) % DEPTH) // BLOCK
    departed = (layer == chosen) & (heading != 0)

    def place(q, row, col):
        return q if (row, col) == (0, 0) else 19 + 3 * q + REST.index((row, col))

    def pack(source, tiles):
        values = []
        for q, row, col in tiles:
            for number in ((1, 2), (3, 0))[col]:
                lanes = slice(number * LANES, (number + 1) * LANES)
                values.append(source[q, 8 * row : 8 * row + 8, lanes])
        moved = [rolled(v, -BLOCK, 1) for v in values]
        values = [jnp.where(chosen == 1, m, v) for m, v in zip(moved, values)]
        moved = [rolled(v, -BLOCK, 1) for v in values]
        values = [jnp.where(first_pick, v, m) for m, v in zip(moved, values)]
        moved = [rolled(v, -2 * BLOCK, 1) for v in values]
        values = [jnp.where(second_pick, v, m) for m, v in zip(moved, values)]
        moved = [rolled(v, 64, 1) for v in values[1::2]]
        for tile, low, high in zip(tiles, values[::2], moved):
            value = jnp.where(tile_lane < 64, low, high)
            east_out[place(*tile)] = jnp.where(heading == 1, value, 0.0)
            west_out[place(*tile)] = jnp.where(heading == -1, value, 0.0)

    def begin(part, first, count):
        span = pl.ds(first, count)
        pair = [
            pltpu.make_async_remote_copy(
                src_ref=source.at[span],
                dst_ref=target.at[span],
                send_sem=move_send.at[part, number],
                recv_sem=move_recv.at[part, number],
                device_id=(wide[number], k),
                device_id_type=MESH,
            )
            for number, (source, target) in enumerate(((east_out, east_in), (west_out, west_in)))
        ]
        for number, copy in enumerate(pair):
            pl.when(in_wide[number])(copy.start)
        return pair

    def cleared(value):
        return jnp.where(jnp.bitwise_and(flags[0, own_rows, own_lanes], 1) != 0, 0.0, value)

    source = post
    for step in range(3):
        for batch in BATCHES:
            values = streamed(source, flags, batch, ROWS, SPAN, own_rows, own_lanes)
            for q, value in zip(batch, values):
                inner[q] = value if step < 2 else rolled(cleared(value), -INNER, 0)
        if step < 2:
            collide(inner, relax, inner_post, SPAN // LANES, ROWS // 8)
            source = inner_post
    for first in range(0, 19, 10):
        pack(inner, [(q, 0, 0) for q in range(first, min(first + 10, 19))])
    started = [begin(0, 0, 19)]

    for n, copy in copies:
        pl.when(behind[n])(copy.wait_recv)

    for i in range(2):
        for j in range(2):
            n = 2 * i + j
            shift = corner_lanes(j, 8)[2]
            for block in range(0, 24, 8):
                value = c_in[n, block : block + 8, :]
                c_full[n, block : block + 8, :] = value
                c_full[n, 24 + block : 32 + block, :] = rolled(value, 2 * DEPTH, 1)
            c_rows[n, 8:16, :] = rolled(c_in[n, 24:32, :], -shift, 1)
            third = corner_lanes(j, 2)[1]
            for m, q in enumerate(CROSS_Y[j]):
                value = c_in[n, 24 + 2 * m : 26 + 2 * m, :] if m < 4 else c_rows[n, 10:12, :]
                rows = slice(2 * q, 2 * q + 2)
                c_full[n, rows, :] = jnp.where(third, value, c_full[n, rows, :])
            rows = slice(44 + SHARED[i][j], 45 + SHARED[i][j])
            third = corner_lanes(j, 1)[1]
            c_full[n, rows, :] = jnp.where(third, c_rows[n, 12:13, :], c_full[n, rows, :])
            c_full[n, 48:49, :] = c_rows[n, 8:9, :]

    for j in range(2):
        lanes = slice(EXT_SPAN - LANES, EXT_SPAN) if j == 0 else slice(SPAN, SPAN + LANES)
        for q in range(19):
            post[q, own_rows, lanes] = y_in[j, q]
    near = slice(SPAN, NEAR_SPAN)

    def merged(above, below):
        here = lax.broadcasted_iota(jnp.int32, above.shape, above.ndim - 1) < 2 * DEPTH
        return jnp.where(here, above, below)

    relax[own_rows, near] = merged(y_relax[1], y_relax[0])
    for plane in range(2):
        flags[plane, own_rows, near] = merged(y_flags[1, plane], y_flags[0, plane])

    for i in range(2):
        rows = slice(22, 24) if i == 0 else slice(16, 18)
        third = slice(21, 22) if i == 0 else slice(18, 19)
        pieces = (
            (x_in.at[i], own_lanes),
            (c_full.at[2 * i], slice(EXT_SPAN - LANES, EXT_SPAN)),
            (c_full.at[2 * i + 1], slice(SPAN, SPAN + LANES)),
        )
        for source, lanes in pieces:
            for q in range(19):
                post[q, rows, lanes] = source[2 * q : 2 * q + 2, :]
            for j, q in enumerate(CROSS_X[i]):
                post[q, third, lanes] = source[44 + j : 45 + j, :]
        pieces = (
            (lambda part: x_in[i, part, :], own_lanes),
            (lambda part: merged(c_full[2 * i + 1, part, :], c_full[2 * i, part, :]), near),
        )
        for source, lanes in pieces:
            relax[rows, lanes] = source(slice(38, 40))
            for plane in range(2):
                bits = source(slice(40 + 2 * plane, 42 + 2 * plane))
                flags[plane, rows, lanes] = bits.astype(jnp.int32)

    for n, copy in copies:
        pl.when(exists[n])(copy.wait_send)

    for span in (EXT_SPAN, NEAR_SPAN):
        for batch in BATCHES:
            for q, value in zip(batch, streamed(post, flags, batch, EXT_ROWS, span, all_rows, near_lanes)):
                state[q, :, near_lanes] = value
        collide(state, relax, post, NEAR_SPAN // LANES, EXT_ROWS // 8)

    for part, pops in enumerate(PARTS):
        for first in range(0, len(pops), 2):
            batch = pops[first : first + 2]
            values = streamed(post, flags, batch, EXT_ROWS, NEAR_SPAN, own_rows, own_lanes)
            for q, value in zip(batch, values):
                value = cleared(value)
                final[q] = jnp.where(departed, 0.0, value)
                state[q, own_rows, own_lanes] = rolled(value, -INNER, 0)
            pack(state, [(q, row, col) for q in batch for row, col in REST])
        started.append(begin(1 + part, 19 + 3 * pops[0], 3 * len(pops)))

    def arrived(part):
        for number, copy in enumerate(started[part]):
            pl.when(in_wide[1 - number])(copy.wait_recv)

    def received(q, row, col):
        east = jnp.where(in_wide[1], east_in[place(q, row, col)], 0.0)
        west = jnp.where(in_wide[0], west_in[place(q, row, col)], 0.0)
        return rolled(east + west, INNER, 0)

    arrived(0)
    for part, pops in enumerate(PARTS):
        arrived(1 + part)
        for first in range(0, len(pops), 2):
            batch = pops[first : first + 2]
            tiles = [[[received(q, row, col) for col in range(2)] for row in range(2)] for q in batch]
            tiles = [
                [
                    [
                        rolled(jnp.where(tile_row < INNER, t[1 - row][col], t[row][col]), 64, 1)
                        for col in range(2)
                    ]
                    for row in range(2)
                ]
                for t in tiles
            ]
            for q, t in zip(batch, tiles):
                for row in range(2):
                    rows = slice(8 * row, 8 * row + 8)
                    guest[q, rows, 0:LANES] = jnp.where(tile_lane < 64, t[row][1], t[row][0])
                    guest[q, rows, LANES:] = jnp.where(tile_lane < 64, t[row][0], t[row][1])
    for pair in started:
        for number, copy in enumerate(pair):
            pl.when(in_wide[number])(copy.wait_send)


def store(final, guest, final_out, guest_out, sems):
    copies = [
        pltpu.make_async_copy(final, final_out, sems.at[0]),
        pltpu.make_async_copy(guest, guest_out, sems.at[1]),
    ]
    for copy in copies:
        copy.start()
    for copy in copies:
        copy.wait()


def local(populations, relaxation, link_flags, migrations):
    populations, relaxation, link_flags, migrations = (
        pltpu.with_memory_space_constraint(operand, pltpu.HBM)
        for operand in (populations, relaxation, link_flags, migrations)
    )
    hbm = pl.BlockSpec(memory_space=pltpu.HBM)
    vmem = pl.BlockSpec(memory_space=pltpu.VMEM)
    f32, i32 = jnp.float32, jnp.int32
    block = (19 * 4, 8, LANES)
    results = pl.pallas_call(
        kernel,
        out_shape=(
            jax.ShapeDtypeStruct((19, ROWS, SPAN), f32),
            jax.ShapeDtypeStruct((19, ROWS, SPAN // 2), f32),
        ),
        in_specs=[hbm] * 4,
        out_specs=(vmem, vmem),
        scratch_shapes=[
            pltpu.VMEM((19, EXT_ROWS, NEAR_SPAN), f32),
            pltpu.VMEM((19, EXT_ROWS, EXT_SPAN), f32),
            pltpu.VMEM((19, ROWS, SPAN), f32),
            pltpu.VMEM((19, ROWS, SPAN), f32),
            pltpu.VMEM((EXT_ROWS, NEAR_SPAN), f32),
            pltpu.VMEM((2, EXT_ROWS, NEAR_SPAN), i32),
            pltpu.SMEM((1, 1, 2), i32),
            pltpu.VMEM((2, MESSAGE, SPAN), f32),
            pltpu.VMEM((2, MESSAGE, SPAN), f32),
            pltpu.VMEM((4, CORNER, LANES), f32),
            pltpu.VMEM((4, CORNER, LANES), f32),
            pltpu.VMEM((4, 16, LANES), f32),
            pltpu.VMEM((4, MESSAGE, LANES), f32),
            pltpu.VMEM((2, 19, ROWS, LANES), f32),
            pltpu.VMEM((2, ROWS, LANES), f32),
            pltpu.VMEM((2, 2, ROWS, LANES), i32),
            pltpu.VMEM(block, f32),
            pltpu.VMEM(block, f32),
            pltpu.VMEM(block, f32),
            pltpu.VMEM(block, f32),
            pltpu.SemaphoreType.DMA((4,)),
            pltpu.SemaphoreType.DMA((12,)),
            pltpu.SemaphoreType.DMA((12,)),
            pltpu.SemaphoreType.DMA((1 + len(PARTS), 2)),
            pltpu.SemaphoreType.DMA((1 + len(PARTS), 2)),
        ],
        compiler_params=pltpu.CompilerParams(
            collective_id=0, has_side_effects=True, vmem_limit_bytes=24 * 1024 * 1024
        ),
        cost_estimate=pl.CostEstimate(
            flops=8_000_000, bytes_accessed=2_000_000, transcendentals=0
        ),
    )(populations, relaxation, link_flags, migrations)
    return pl.pallas_call(
        store,
        out_shape=tuple(jax.ShapeDtypeStruct(r.shape, f32) for r in results),
        in_specs=[vmem] * 2,
        out_specs=(hbm, hbm),
        scratch_shapes=[pltpu.SemaphoreType.DMA((2,))],
        compiler_params=pltpu.CompilerParams(vmem_limit_bytes=8 * 1024 * 1024),
    )(*results)


def solution(mesh):
    placed = (
        P(None, "wide", "cross"),
        P("wide", "cross"),
        P(None, "wide", "cross"),
        P("wide", "cross", None),
    )
    return jax.shard_map(
        local,
        mesh=mesh,
        in_specs=placed,
        out_specs=(P(None, "wide", "cross"), P(None, "wide", "cross")),
        check_vma=False,
    )
```
